128 devices in a mesh: rep: 2 (over core), seq: 64 (over y, x, z).
Axes of the slice: x: 4, y: 4, z: 4, core: 2. Of those that a mesh axis runs over, the one named last changes fastest.
Arguments:
- queries: bfloat16 [16384, 8192], P(('rep', 'seq')), parts along dimension 0, may hold values from -180 to 180
- keys: bfloat16 [65536, 1024], P(('rep', 'seq')), parts along dimension 0, may hold values from -6 to 6
- values: bfloat16 [65536, 1024], P(('rep', 'seq')), parts along dimension 0, may hold values from -6 to 6
- vertical: int32 [128, 64], P('rep'), parts along dimension 0, may hold values from 0 to 511, all different within a row
- vert_count: int32 [128], P('rep'), parts along dimension 0, may hold values from 1 to 64
- slash: int32 [128, 32], P('rep'), parts along dimension 0, may hold values from 0 to 383, all different within a row
- slash_count: int32 [128], P('rep'), parts along dimension 0, may hold values from 1 to 32
Outputs:
- attended: bfloat16 [16384, 8192], P(('rep', 'seq')), parts along dimension 0
The draws below stay inside these ranges and needn't reach their ends.
There are 2 independent parts, one for each index of `rep`. The reference program is written for one: setup_inputs(seed, part) draws one part's arguments, and reference() takes and returns one part's arrays. A program takes and returns all parts, laid end to end along the dimension named above; each array names one. Nothing has to cross between parts.
Inputs may be any that keep to these rules, and one draw needn't show every extreme that they name: `vertical`: each row holds 64 different key block numbers; head h uses the first vert_count[h] of them. `slash`: each row holds 32 different numbers; head h uses the first slash_count[h] of them, each number s naming the slash offset s + 1 blocks.
All inputs are finite; a program needn't handle non-finite values.
Results may differ from the reference program's by a relative error of at most 0.007.
Values may be sent and summed in bfloat16 or wider, within the bound.
A program may use at most 128 MiB of HBM per device.

```python
import math
import jax
import jax.numpy as jnp
from jax import lax

QUERY_HEADS = 64
KV_HEADS = 8
HEAD_DIM = 128
BLOCK = 64
VERT = 64
SLASHES = 32
QUERIES = 8192
CONTEXT = 32768
QBLOCKS = 128
KBLOCKS = 512
SPAN = 384


def make_pair(key):
    base_keys = jnp.clip(jax.random.normal(jax.random.fold_in(key, 101), (CONTEXT, KV_HEADS, HEAD_DIM), jnp.float32), -6.0, 6.0)
    base_queries = jnp.clip(jax.random.normal(jax.random.fold_in(key, 102), (QUERIES, QUERY_HEADS, HEAD_DIM), jnp.float32), -6.0, 6.0)
    return (base_queries.reshape(QUERIES, QUERY_HEADS * HEAD_DIM), base_keys.reshape(CONTEXT, KV_HEADS * HEAD_DIM))


def draw_queries(key, part):
    return make_pair(key)[0].astype(jnp.bfloat16)


def draw_keys(key, part):
    return make_pair(key)[1].astype(jnp.bfloat16)


def set_ends(entries, stream_key, smallest, high):
    index_at = [jax.random.randint(jax.random.fold_in(stream_key, axis), (), 0, length) for axis, length in enumerate(entries.shape)]
    longest = entries.shape.index(max(entries.shape))
    neighbour = index_at[:longest] + [(index_at[longest] + 1) % entries.shape[longest]] + index_at[longest + 1:]
    return entries.at[tuple(index_at)].set(smallest).at[tuple(neighbour)].set(high)


def block_levels(rng, extent, split, smallest, top_value):
    loudness = 1.0
    for axis_at, blocks in split:
        heights = jax.random.uniform(jax.random.fold_in(jax.random.fold_in(rng, 6), axis_at), (blocks,), jnp.float32, smallest / len(split), top_value / len(split))
        loudness = loudness * jnp.repeat(jnp.exp(heights), extent[axis_at] // blocks).reshape((-1,) + (1,) * (len(extent) - 1 - axis_at))
    return loudness


def distinct(own_key, rows, count, top, lift):
    order = jax.random.permutation(jax.random.fold_in(own_key, 1), count)
    favour = order
    for power in range(3):
        favour = favour * favour // count
    favour = favour * lift // count
    chance = jax.random.randint(jax.random.fold_in(own_key, 2), (rows, count), 0, 4096) + favour
    holders = jax.random.permutation(jax.random.fold_in(own_key, 3), rows)[jnp.arange(count) % rows]
    chance = jnp.where(jnp.arange(rows)[:, None] == holders[None, :], 1 << 14, chance)
    score = chance * count + jnp.arange(count)
    return lax.top_k(score.astype(jnp.int32), top)[1].astype(jnp.int32)


def scatter_about(rng, extent, scale, bound, split=(), kind=jnp.bfloat16):
    values = jax.random.normal(rng, extent, jnp.float32) * scale
    if len(split) > 0:
        values = block_levels(rng, extent, split, -0.22, 0.18) * values
    return jnp.clip(values, min=-bound, max=bound).astype(kind)


def setup_inputs(seed: int = 0, part: int = 0) -> dict:
    seeds = jax.random.split(jax.random.key(seed), 8)
    part_splits = jax.random.split(jax.random.fold_in(seeds[7], part), 8)
    queries = draw_queries(jax.random.fold_in(jax.random.fold_in(seeds[7], part), 71), part)
    keys = draw_keys(jax.random.fold_in(jax.random.fold_in(seeds[7], part), 71), part)
    values = scatter_about(part_splits[2], (CONTEXT, KV_HEADS * HEAD_DIM), 1.0, 6.0, ((0, 64),))
    vertical = distinct(part_splits[3], QUERY_HEADS, KBLOCKS, VERT, 0)
    vert_count = set_ends(jax.random.randint(part_splits[4], (QUERY_HEADS,), 1, VERT + 1), jax.random.fold_in(part_splits[4], 1), 1, VERT).astype(jnp.int32)
    slash = distinct(part_splits[5], QUERY_HEADS, SPAN, SLASHES, 0)
    slash_count = set_ends(jax.random.randint(part_splits[6], (QUERY_HEADS,), 1, SLASHES + 1), jax.random.fold_in(part_splits[6], 1), 1, SLASHES).astype(jnp.int32)
    return {"queries": queries, "keys": keys, "values": values, "vertical": vertical, "vert_count": vert_count, "slash": slash, "slash_count": slash_count}


def reference(queries, keys, values, vertical, vert_count, slash, slash_count):
    per_group = QUERY_HEADS // KV_HEADS
    query_grid = queries.reshape(QBLOCKS, BLOCK, QUERY_HEADS, HEAD_DIM)
    key_grid = keys.reshape(KBLOCKS, BLOCK, KV_HEADS, HEAD_DIM)
    value_grid = values.reshape(KBLOCKS, BLOCK, KV_HEADS, HEAD_DIM)
    absolute = (KBLOCKS - QBLOCKS + jnp.arange(QBLOCKS, dtype=jnp.int32)).astype(jnp.int32)
    scale = 1.0 / math.sqrt(HEAD_DIM)
    causal = jnp.arange(BLOCK)[:, None] >= jnp.arange(BLOCK)[None, :]
    exact = lax.Precision.HIGHEST

    def one_head(head):
        group = head // per_group
        query = jnp.take(query_grid, head, axis=2).astype(jnp.float32)
        key_set = jnp.take(key_grid, group, axis=2)
        value_set = jnp.take(value_grid, group, axis=2)
        verticals = vertical[head]
        live_vert = vert_count[head]
        offsets = (slash[head] + 1).astype(jnp.int32)
        live_slash = slash_count[head]
        marks = jnp.arange(VERT, dtype=jnp.int32) < live_vert
        target = (absolute[:, None] - offsets[None, :]).astype(jnp.int32)
        own_keys = key_set[absolute].astype(jnp.float32)
        own_values = value_set[absolute].astype(jnp.float32)
        vert_keys = key_set[verticals].reshape(VERT * BLOCK, HEAD_DIM).astype(jnp.float32)
        vert_values = value_set[verticals].reshape(VERT * BLOCK, HEAD_DIM).astype(jnp.float32)
        slash_keys = key_set[target].reshape(QBLOCKS, SLASHES * BLOCK, HEAD_DIM).astype(jnp.float32)
        slash_values = value_set[target].reshape(QBLOCKS, SLASHES * BLOCK, HEAD_DIM).astype(jnp.float32)
        own_scores = jnp.einsum('rqd,rkd->rqk', query, own_keys, precision=exact) * scale
        vert_scores = jnp.einsum('rqd,kd->rqk', query, vert_keys, precision=exact) * scale
        slash_scores = jnp.einsum('rqd,rkd->rqk', query, slash_keys, precision=exact) * scale
        vert_ok = marks[None, :] & (verticals[None, :] < absolute[:, None])
        covered = jnp.any((target[:, :, None] == verticals[None, None, :]) & marks[None, None, :], axis=2)
        slash_ok = (jnp.arange(SLASHES, dtype=jnp.int32) < live_slash)[None, :] & jnp.logical_not(covered)
        own_valid = jnp.broadcast_to(causal[None], (QBLOCKS, BLOCK, BLOCK))
        vert_valid = jnp.broadcast_to(jnp.repeat(vert_ok, BLOCK, axis=1)[:, None, :], (QBLOCKS, BLOCK, VERT * BLOCK))
        slash_valid = jnp.broadcast_to(jnp.repeat(slash_ok, BLOCK, axis=1)[:, None, :], (QBLOCKS, BLOCK, SLASHES * BLOCK))
        scores = jnp.concatenate([own_scores, vert_scores, slash_scores], axis=2)
        valid = jnp.concatenate([own_valid, vert_valid, slash_valid], axis=2)
        scores = jnp.where(valid, scores, -jnp.inf)
        peak = lax.optimization_barrier(jnp.max(scores, axis=2, keepdims=True))
        weights = jnp.exp(scores - peak)
        total = lax.optimization_barrier(jnp.sum(weights, axis=2, keepdims=True))
        rounded = lax.optimization_barrier(weights.astype(jnp.bfloat16)).astype(jnp.float32)
        first_cut = BLOCK
        second_cut = BLOCK + VERT * BLOCK
        result = jnp.einsum('rqk,rkd->rqd', rounded[:, :, :first_cut], own_values, precision=exact)
        result = result + jnp.einsum('rqk,kd->rqd', rounded[:, :, first_cut:second_cut], vert_values, precision=exact)
        result = result + jnp.einsum('rqk,rkd->rqd', rounded[:, :, second_cut:], slash_values, precision=exact)
        return (result / total).astype(jnp.bfloat16)
    heads = lax.map(one_head, jnp.arange(QUERY_HEADS, dtype=jnp.int32))
    return heads.transpose(1, 2, 0, 3).reshape(QUERIES, QUERY_HEADS * HEAD_DIM)
```

```python
import functools, math
import jax, jax.numpy as jnp
from jax import lax
from jax.experimental import pallas as pl
from jax.experimental.pallas import tpu as pltpu
from jax.sharding import PartitionSpec as P

KV_HEADS = 8
HEAD_DIM = 128
D = HEAD_DIM
BLOCK = 64
VERT = 64
SLOTS=36
VT=8
ST=4
R=256
NEG=float("-inf")

def attn_kernel(sv, isv, offs, meta, qb, q_ref, kv_ref, o_ref, kvv, s_v, s_s, mx, acc, sm):
    h = pl.program_id(0)
    n_eff, n_full, ns = meta[0, h], meta[1, h], meta[2, h]
    vtiles = (n_eff + VT - 1) // VT
    ftiles = n_full // VT
    stiles = (ns + 1 + ST - 1) // ST
    c = math.log2(math.e) / math.sqrt(D)
    last = kv_ref.shape[0] // BLOCK - 1

    def gather(i, _):
        for u in range(VT):
            b = jnp.minimum(sv[h, i * VT + u], last)
            kvv[pl.ds((i * VT + u) * BLOCK, BLOCK), :] = kv_ref[pl.ds(b * BLOCK, BLOCK), :]
        return 0
    lax.fori_loop(0, vtiles, gather, 0)
    lane = lax.broadcasted_iota(jnp.int32, (1, 128), 1)
    low = lane < BLOCK
    nsub = R // BLOCK

    def two(x, y):
        return jnp.where(low, x, y)

    def row_tile(rt, _):
        q = q_ref[pl.ds(rt * R, R), :]
        blocks = [qb[rt * nsub + i] for i in range(nsub)]
        mx[...] = jnp.full_like(mx, NEG)

        def va(t, masked):
            k = kvv[pl.ds(t * VT * BLOCK, VT * BLOCK), 0:D]
            s = lax.dot_general(q, k, (((1,), (1,)), ((), ())), preferred_element_type=jnp.float32)
            if masked:
                ids = [sv[h, t * VT + u] for u in range(VT)]
                rows = []
                for i in range(nsub):
                    cols = []
                    for cg in range(VT // 2):
                        b = two(jnp.where(ids[2 * cg] < blocks[i], 0.0, NEG), jnp.where(ids[2 * cg + 1] < blocks[i], 0.0, NEG))
                        cols.append(s[i * BLOCK:(i + 1) * BLOCK, cg * 128:(cg + 1) * 128] + b)
                    rows.append(jnp.concatenate(cols, axis=1))
                s = jnp.concatenate(rows, axis=0)
            s_v[:, pl.ds(pl.multiple_of(t * VT * BLOCK, VT * BLOCK), VT * BLOCK)] = s
            m = s[:, 0:128]
            for cg in range(1, VT // 2):
                m = jnp.maximum(m, s[:, cg * 128:(cg + 1) * 128])
            mx[...] = jnp.maximum(mx[...], m)

        lax.fori_loop(0, ftiles, lambda t, _: (va(t, False), 0)[1], 0)
        lax.fori_loop(ftiles, vtiles, lambda t, _: (va(t, True), 0)[1], 0)

        def slots_of(t, i):
            return [blocks[i] - offs[h, t * ST + u] for u in range(ST)]

        def sa(t, first):
            for i in range(nsub):
                js = slots_of(t, i)
                k = jnp.concatenate([kv_ref[pl.ds(j * BLOCK, BLOCK), 0:D] for j in js], axis=0)
                s = lax.dot_general(q[i * BLOCK:(i + 1) * BLOCK], k, (((1,), (1,)), ((), ())), preferred_element_type=jnp.float32)
                m = mx[i * BLOCK:(i + 1) * BLOCK, :]
                for cg in range(ST // 2):
                    bias = []
                    for u in (2 * cg, 2 * cg + 1):
                        dead = jnp.where(t * ST + u <= ns, isv[h, js[u]], 1)
                        if first and u == 0:
                            dead = 0
                        bias.append(jnp.where(dead == 0, 0.0, NEG))
                    part = s[:, cg * 128:(cg + 1) * 128] + two(*bias)
                    if first and cg == 0:
                        ri = lax.broadcasted_iota(jnp.int32, (BLOCK, 128), 0)
                        ci = lax.broadcasted_iota(jnp.int32, (BLOCK, 128), 1)
                        part = jnp.where((ci >= BLOCK) | (ri >= ci), part, NEG)
                    s_s[i * BLOCK:(i + 1) * BLOCK, pl.ds(pl.multiple_of(t * ST * BLOCK + cg * 128, 128), 128)] = part
                    m = jnp.maximum(m, part)
                mx[i * BLOCK:(i + 1) * BLOCK, :] = m
        sa(0, True)
        lax.fori_loop(1, stiles, lambda t, _: (sa(t, False), 0)[1], 0)

        mrow = jnp.max(mx[...], axis=1, keepdims=True)
        mx[...] = jnp.broadcast_to(mrow * c, (R, 128))
        sm[...] = jnp.zeros_like(sm)
        acc[...] = jnp.zeros_like(acc)

        def vb(t, _):
            v = kvv[pl.ds(t * VT * BLOCK, VT * BLOCK), D:2 * D]
            mc = mx[...]
            ps = []
            tot = None
            for cg in range(VT // 2):
                s = s_v[:, pl.ds(pl.multiple_of(t * VT * BLOCK + cg * 128, 128), 128)]
                p = jnp.exp2(s * c - mc)
                tot = p if tot is None else tot + p
                ps.append(p.astype(jnp.bfloat16))
            sm[...] += tot
            acc[...] += jnp.dot(jnp.concatenate(ps, axis=1), v, preferred_element_type=jnp.float32)
            return 0
        lax.fori_loop(0, vtiles, vb, 0)

        def sb(t, _):
            for i in range(nsub):
                js = slots_of(t, i)
                rows = slice(i * BLOCK, (i + 1) * BLOCK)
                v = jnp.concatenate([kv_ref[pl.ds(j * BLOCK, BLOCK), D:2 * D] for j in js], axis=0)
                mc = mx[rows, :]
                ps = []
                tot = sm[rows, :]
                for cg in range(ST // 2):
                    s = s_s[rows, pl.ds(pl.multiple_of(t * ST * BLOCK + cg * 128, 128), 128)]
                    p = jnp.exp2(s * c - mc)
                    tot = tot + p
                    ps.append(p.astype(jnp.bfloat16))
                sm[rows, :] = tot
                acc[rows, :] += jnp.dot(jnp.concatenate(ps, axis=1), v, preferred_element_type=jnp.float32)
            return 0
        lax.fori_loop(0, stiles, sb, 0)
        total = jnp.sum(sm[...], axis=1, keepdims=True)
        o_ref[pl.ds(rt * R, R), :] = (acc[...] / total).astype(o_ref.dtype)
        return 0
    lax.fori_loop(0, q_ref.shape[0] // R, row_tile, 0)


def attend(tables, q, kv):
    rows, cols = q.shape
    heads = cols // D
    return pl.pallas_call(
        attn_kernel,
        grid_spec=pltpu.PrefetchScalarGridSpec(
            num_scalar_prefetch=5,
            grid=(heads,),
            in_specs=[pl.BlockSpec((rows, D), lambda h, *_: (0, h)),
                      pl.BlockSpec(memory_space=pltpu.VMEM)],
            out_specs=pl.BlockSpec((rows, D), lambda h, *_: (0, h)),
            scratch_shapes=[
                pltpu.VMEM((VERT * BLOCK, 2 * D), jnp.bfloat16),
                pltpu.VMEM((R, VERT * BLOCK), jnp.float32),
                pltpu.VMEM((R, SLOTS * BLOCK), jnp.float32),
                pltpu.VMEM((R, 128), jnp.float32),
                pltpu.VMEM((R, D), jnp.float32),
                pltpu.VMEM((R, 128), jnp.float32),
            ],
        ),
        out_shape=jax.ShapeDtypeStruct((rows, cols), jnp.bfloat16),
        compiler_params=pltpu.CompilerParams(vmem_limit_bytes=56 << 20),
    )(*tables, q, kv)


def tables_of(vertical, vert_count, slash, slash_count, blocks, context_blocks, query_blocks):
    n = vertical.shape[1]
    idx = jnp.arange(n, dtype=jnp.int32)
    live = idx[None] < vert_count[:, None]
    key = jnp.where(live, vertical, 4096 + idx[None])
    rank = jnp.sum((key[:, None, :] < key[:, :, None]).astype(jnp.int32), axis=2)
    sv = jnp.sum(jnp.where(rank[:, :, None] == idx[None, None, :], key[:, :, None], 0), axis=1)
    n_eff = jnp.sum((key < jnp.max(blocks)).astype(jnp.int32), axis=1)
    n_full = jnp.sum((key < jnp.min(blocks)).astype(jnp.int32), axis=1)
    isv = jnp.sum((key[:, :, None] == jnp.arange(context_blocks, dtype=jnp.int32)[None, None]).astype(jnp.int32), axis=1)
    offs = jnp.pad(slash + 1, ((0, 0), (1, SLOTS - 1 - slash.shape[1])))
    meta = jnp.stack([n_eff, n_full, slash_count])
    return sv, isv, offs, meta, blocks


MESH_ID = pl.DeviceIdType.MESH
PEERS = 8
LATE = (5, 6, 7)


def place():
    rep = lax.axis_index("rep")
    seq = lax.axis_index("seq")
    y, x, z = seq // 16, (seq // 4) % 4, seq % 4
    ring = y * (1 - rep) + z * rep
    other = z * (1 - rep) + y * rep
    shifted = (x + rep) % 4
    half, low = shifted // 2, shifted % 2
    return rep, seq, ring, half, low, other


def seq_at(rep, ring, half, low, other):
    y = ring * (1 - rep) + other * rep
    z = other * (1 - rep) + ring * rep
    x = (2 * half + low + 4 - rep) % 4
    return y * 16 + x * 4 + z


def peer_seq(rep, ring, turn, group):
    half, other = group // 4, group % 4
    return seq_at(rep, ring, half, (turn + half) % 2, other)


def aligned(index, size):
    return pl.ds(pl.multiple_of(index * size, size), size)


def spread_kernel(keys, values, queries, kv, q_out, local_sem, first_send, first_recv, tree_send, tree_recv):
    rep, seq, ring, half, low, other = place()
    group = half * 4 + other
    turn = (low + half) % 2
    rows = keys.shape[0]
    q_rows = queries.shape[0]
    q_width = q_out.shape[1]

    peers = [(rep, peer_seq(rep, ring, turn, (group + d) % PEERS)) for d in range(1, PEERS)]
    neighbours = {
        "pair": (rep, seq_at(rep, ring, half, 1 - low, other)),
        "up": (rep, seq_at(rep, (ring + 1) % 4, half, low, other)),
        "down": (rep, seq_at(rep, (ring + 3) % 4, half, low, other)),
    }
    barrier = pltpu.get_barrier_semaphore()
    for device in peers + list(neighbours.values()):
        pl.semaphore_signal(barrier, inc=1, device_id=device, device_id_type=MESH_ID)
    pl.semaphore_wait(barrier, len(peers) + len(neighbours))

    def first(d, kind):
        to = (group + d) % PEERS
        source = keys if kind == 0 else values
        return pltpu.make_async_remote_copy(
            src_ref=source.at[:, aligned(to, HEAD_DIM)],
            dst_ref=kv.at[aligned(seq, rows), pl.ds(kind * HEAD_DIM, HEAD_DIM)],
            send_sem=first_send.at[d, kind],
            recv_sem=first_recv.at[d, kind],
            device_id=peers[d - 1],
            device_id_type=MESH_ID,
        )

    def first_q(d):
        to = (group + d) % PEERS
        return pltpu.make_async_remote_copy(
            src_ref=queries.at[:, aligned(to, q_width)],
            dst_ref=q_out.at[aligned(group, q_rows), :],
            send_sem=first_send.at[d, 2],
            recv_sem=first_recv.at[d, 2],
            device_id=peers[d - 1],
            device_id_type=MESH_ID,
        )

    own = [
        pltpu.make_async_copy(keys.at[:, aligned(group, HEAD_DIM)], kv.at[aligned(seq, rows), pl.ds(0, HEAD_DIM)], local_sem.at[0]),
        pltpu.make_async_copy(values.at[:, aligned(group, HEAD_DIM)], kv.at[aligned(seq, rows), pl.ds(HEAD_DIM, HEAD_DIM)], local_sem.at[1]),
        pltpu.make_async_copy(queries.at[:, aligned(group, q_width)], q_out.at[aligned(group, q_rows), :], local_sem.at[2]),
    ]
    own[0].start()
    own[1].start()
    for d in range(1, PEERS):
        first(d, 0).start()
        first(d, 1).start()
    own[2].start()
    for d in range(1, PEERS):
        first_q(d).start()

    def piece_rows(up, flip, d):
        origin_low = (low + flip) % 2
        origin_turn = (origin_low + half) % 2
        origin_ring = (ring + 4 - up) % 4
        return aligned(peer_seq(rep, origin_ring, origin_turn, (group + PEERS - d) % PEERS), rows)

    moves = {"pair": (0, 1), "up": (1, 0), "down": (3, 0)}
    sends = []

    def pass_on(up, flip, d, way):
        step_up, step_flip = moves[way]
        at = piece_rows(up, flip, d)
        copy = pltpu.make_async_remote_copy(
            src_ref=kv.at[at, :],
            dst_ref=kv.at[at, :],
            send_sem=tree_send.at[len(sends)],
            recv_sem=tree_recv.at[(up + step_up) % 4, (flip + step_flip) % 2, d],
            device_id=neighbours[way],
            device_id_type=MESH_ID,
        )
        copy.start()
        sends.append(copy)

    def arrived(up, flip, d):
        at = piece_rows(up, flip, d)
        pltpu.make_async_remote_copy(
            src_ref=kv.at[at, :],
            dst_ref=kv.at[at, :],
            send_sem=tree_send.at[0],
            recv_sem=tree_recv.at[up, flip, d],
            device_id=neighbours["pair"],
            device_id_type=MESH_ID,
        ).wait_recv()

    actions = []
    for d in range(PEERS):
        onward = "up" if d % 2 == 0 else "down"
        turning = 1 if d % 2 == 0 else 3
        late = d in LATE
        actions.append((d, 0, 0, d, ["up", "down", "pair"]))
        for up in (1, 3):
            ways = [onward] if up == turning else []
            actions.append((d + 1, up, 0, d, ways + (["pair"] if late else [])))
            actions.append((d + 2, up, 1, d, [] if late else ways))
        actions.append((d + 2, 2, 0, d, ["pair"] if late else []))
        actions.append((d + 1, 0, 1, d, [] if late else ["up", "down"]))
        actions.append((d + 3, 2, 1, d, []))
    ends = [a for a in actions if not a[4]]
    for _, up, flip, d, ways in sorted(a for a in actions if a[4]):
        if (up, flip) != (0, 0):
            arrived(up, flip, d)
        elif d == 0:
            own[0].wait()
            own[1].wait()
        else:
            first(d, 0).wait_recv()
            first(d, 1).wait_recv()
        for way in ways:
            pass_on(up, flip, d, way)
    for _, up, flip, d, _ in ends:
        arrived(up, flip, d)
    own[2].wait()
    for d in range(1, PEERS):
        first_q(d).wait_recv()
    for d in range(1, PEERS):
        first(d, 0).wait_send()
        first(d, 1).wait_send()
        first_q(d).wait_send()
    for copy in sends:
        copy.wait_send()


def spread(keys, values, queries):
    seq_count = lax.axis_size("seq")
    any_space = pl.BlockSpec(memory_space=pl.ANY)
    return pl.pallas_call(
        spread_kernel,
        out_shape=(
            jax.ShapeDtypeStruct((seq_count * keys.shape[0], 2 * HEAD_DIM), keys.dtype),
            jax.ShapeDtypeStruct((PEERS * queries.shape[0], queries.shape[1] // PEERS), queries.dtype),
        ),
        in_specs=[any_space] * 3,
        out_specs=(any_space, any_space),
        scratch_shapes=[
            pltpu.SemaphoreType.DMA((3,)),
            pltpu.SemaphoreType.DMA((PEERS, 3)),
            pltpu.SemaphoreType.DMA((PEERS, 3)),
            pltpu.SemaphoreType.DMA((56,)),
            pltpu.SemaphoreType.DMA((4, 2, PEERS)),
        ],
        compiler_params=pltpu.CompilerParams(collective_id=0, has_side_effects=True),
        name="spread",
    )(keys, values, queries)


def give_back_kernel(result, out, local_sem, send_sem, recv_sem):
    rep, seq, ring, half, low, other = place()
    group = half * 4 + other
    turn = (low + half) % 2
    rows, width = out.shape[0], result.shape[1]
    peers = [(rep, peer_seq(rep, ring, turn, (group + d) % PEERS)) for d in range(1, PEERS)]
    barrier = pltpu.get_barrier_semaphore()
    for device in peers:
        pl.semaphore_signal(barrier, inc=1, device_id=device, device_id_type=MESH_ID)
    pl.semaphore_wait(barrier, len(peers))
    copies = []
    for d in range(1, PEERS):
        copy = pltpu.make_async_remote_copy(
            src_ref=result.at[aligned((group + d) % PEERS, rows), :],
            dst_ref=out.at[:, aligned(group, width)],
            send_sem=send_sem.at[d],
            recv_sem=recv_sem.at[d],
            device_id=peers[d - 1],
            device_id_type=MESH_ID,
        )
        copy.start()
        copies.append(copy)
    own = pltpu.make_async_copy(result.at[aligned(group, rows), :], out.at[:, aligned(group, width)], local_sem)
    own.start()
    own.wait()
    for d in range(1, PEERS):
        pltpu.make_async_remote_copy(
            src_ref=result.at[aligned((group + d) % PEERS, rows), :],
            dst_ref=out.at[:, aligned((group + PEERS - d) % PEERS, width)],
            send_sem=send_sem.at[d],
            recv_sem=recv_sem.at[d],
            device_id=peers[d - 1],
            device_id_type=MESH_ID,
        ).wait_recv()
    for copy in copies:
        copy.wait_send()


def give_back(result, rows):
    any_space = pl.BlockSpec(memory_space=pl.ANY)
    return pl.pallas_call(
        give_back_kernel,
        out_shape=jax.ShapeDtypeStruct((rows, PEERS * result.shape[1]), result.dtype),
        in_specs=[any_space],
        out_specs=any_space,
        scratch_shapes=[
            pltpu.SemaphoreType.DMA,
            pltpu.SemaphoreType.DMA((PEERS,)),
            pltpu.SemaphoreType.DMA((PEERS,)),
        ],
        compiler_params=pltpu.CompilerParams(collective_id=1, has_side_effects=True),
        name="give_back",
    )(result)


def body(queries, keys, values, vertical, vert_count, slash, slash_count):
    rep, seq, ring, half, low, other = place()
    group = half * 4 + other
    turn = (low + half) % 2
    query_rows = queries.shape[0]
    per_device = query_rows // BLOCK
    seq_count = lax.axis_size("seq")
    context_blocks = seq_count * keys.shape[0] // BLOCK
    stretch_blocks = seq_count * per_device
    sources = peer_seq(rep, ring, turn, jnp.arange(PEERS, dtype=jnp.int32))
    blocks = (context_blocks - stretch_blocks + per_device * sources[:, None] + jnp.arange(per_device, dtype=jnp.int32)[None]).reshape(-1)
    per_group = vertical.shape[0] // KV_HEADS

    def mine(x):
        return lax.dynamic_slice_in_dim(x, group * per_group, per_group, 0)

    tables = tables_of(mine(vertical), mine(vert_count), mine(slash), mine(slash_count), blocks, context_blocks, stretch_blocks)
    kv, q = spread(keys, values, queries)
    return give_back(attend(tables, q, kv), query_rows)


def solution(mesh):
    return jax.shard_map(
        body,
        mesh=mesh,
        in_specs=(
            P(("rep", "seq"), None),
            P(("rep", "seq"), None),
            P(("rep", "seq"), None),
            P("rep", None),
            P("rep"),
            P("rep", None),
            P("rep"),
        ),
        out_specs=P(("rep", "seq"), None),
        check_vma=False,
    )
```

```python
import functools, math
import jax, jax.numpy as jnp
from jax import lax
from jax.experimental import pallas as pl
from jax.experimental.pallas import tpu as pltpu
from jax.sharding import PartitionSpec as P

KV_HEADS = 8
HEAD_DIM = 128
D = HEAD_DIM
BLOCK = 64
VERT = 64
SLOTS=40
VT=8
ST=4
R=1024
SPANS = (4, 2, 1)
FIRST = 2
SLASH_SPANS = (4, 2, 1)
NEG=float("-inf")

def attn_kernel(sv, isv, offs, meta, qb, q_ref, kv_ref, o_ref, kvv, s_v, s_s, mx, acc, sm):
    h = pl.program_id(0)
    n_eff, ns = meta[0, h], meta[1, h]
    vtiles = (n_eff + VT - 1) // VT
    stiles = (ns + 1 + ST - 1) // ST
    c = math.log2(math.e) / math.sqrt(D)
    last = kv_ref.shape[0] // BLOCK - 1

    def gather(i, _):
        for u in range(VT):
            b = jnp.minimum(sv[h, i * VT + u], last)
            kvv[pl.ds((i * VT + u) * BLOCK, BLOCK), :] = kv_ref[pl.ds(b * BLOCK, BLOCK), :]
        return 0
    lax.fori_loop(0, vtiles, gather, 0)
    lane = lax.broadcasted_iota(jnp.int32, (1, 128), 1)
    low = lane < BLOCK
    nsub = R // BLOCK

    def two(x, y):
        return jnp.where(low, x, y)

    def row_tile(rt, _):
        q = q_ref[pl.ds(rt * R, R), :]
        blocks = [qb[rt * nsub + i] for i in range(nsub)]
        mx[...] = jnp.full_like(mx, NEG)

        def va(t, span):
            keys = span * VT * BLOCK
            at = pl.ds(pl.multiple_of(t * VT * BLOCK, VT * BLOCK), keys)
            s = lax.dot_general(q, kvv[at, 0:D], (((1,), (1,)), ((), ())), preferred_element_type=jnp.float32)
            ids = [sv[h, t * VT + u] for u in range(span * VT)]
            rows = []
            for i in range(nsub):
                cols = []
                for cg in range(span * VT // 2):
                    b = two(jnp.where(ids[2 * cg] < blocks[i], 0.0, NEG), jnp.where(ids[2 * cg + 1] < blocks[i], 0.0, NEG))
                    cols.append(s[i * BLOCK:(i + 1) * BLOCK, cg * 128:(cg + 1) * 128] + b)
                rows.append(jnp.concatenate(cols, axis=1))
            s = jnp.concatenate(rows, axis=0)
            s_v[:, at] = s
            m = s[:, 0:128]
            for cg in range(1, span * VT // 2):
                m = jnp.maximum(m, s[:, cg * 128:(cg + 1) * 128])
            mx[...] = jnp.maximum(mx[...], m)

        def over_tiles(step):
            done = 0
            for span in SPANS:
                count = (vtiles - done) // span
                lax.fori_loop(0, count, lambda n, _, done=done, span=span: (step(done + n * span, span), 0)[1], 0)
                done = done + count * span

        over_tiles(va)

        def slots_of(t, i, span):
            return [blocks[i] - offs[h, t * ST + u] for u in range(span * ST)]

        def sa(t, span, first=False):
            for i in range(nsub):
                js = slots_of(t, i, span)
                k = jnp.concatenate([kv_ref[pl.ds(j * BLOCK, BLOCK), 0:D] for j in js], axis=0)
                s = lax.dot_general(q[i * BLOCK:(i + 1) * BLOCK], k, (((1,), (1,)), ((), ())), preferred_element_type=jnp.float32)
                m = mx[i * BLOCK:(i + 1) * BLOCK, :]
                for cg in range(span * ST // 2):
                    bias = []
                    for u in (2 * cg, 2 * cg + 1):
                        dead = jnp.where(t * ST + u <= ns, isv[h, js[u]], 1)
                        if first and u == 0:
                            dead = 0
                        bias.append(jnp.where(dead == 0, 0.0, NEG))
                    part = s[:, cg * 128:(cg + 1) * 128] + two(*bias)
                    if first and cg == 0:
                        ri = lax.broadcasted_iota(jnp.int32, (BLOCK, 128), 0)
                        ci = lax.broadcasted_iota(jnp.int32, (BLOCK, 128), 1)
                        part = jnp.where((ci >= BLOCK) | (ri >= ci), part, NEG)
                    s_s[i * BLOCK:(i + 1) * BLOCK, pl.ds(pl.multiple_of(t * ST * BLOCK + cg * 128, 128), 128)] = part
                    m = jnp.maximum(m, part)
                mx[i * BLOCK:(i + 1) * BLOCK, :] = m

        def over_slots(step, done):
            for span in SLASH_SPANS:
                count = jnp.maximum(stiles - done, 0) // span
                lax.fori_loop(0, count, lambda n, _, done=done, span=span: (step(done + n * span, span), 0)[1], 0)
                done = done + count * span

        sa(0, FIRST, True)
        over_slots(sa, FIRST)

        mrow = jnp.max(mx[...], axis=1, keepdims=True)
        mx[...] = jnp.broadcast_to(mrow * c, (R, 128))
        sm[...] = jnp.zeros_like(sm)
        acc[...] = jnp.zeros_like(acc)

        def vb(t, span):
            keys = span * VT * BLOCK
            v = kvv[pl.ds(pl.multiple_of(t * VT * BLOCK, VT * BLOCK), keys), D:2 * D]
            mc = mx[...]
            ps = []
            tot = None
            for cg in range(keys // 128):
                s = s_v[:, pl.ds(pl.multiple_of(t * VT * BLOCK + cg * 128, 128), 128)]
                p = jnp.exp2(s * c - mc)
                tot = p if tot is None else tot + p
                ps.append(p.astype(jnp.bfloat16))
            sm[...] += tot
            acc[...] += jnp.dot(jnp.concatenate(ps, axis=1), v, preferred_element_type=jnp.float32)
        over_tiles(vb)

        def sb(t, span):
            for i in range(nsub):
                js = slots_of(t, i, span)
                rows = slice(i * BLOCK, (i + 1) * BLOCK)
                v = jnp.concatenate([kv_ref[pl.ds(j * BLOCK, BLOCK), D:2 * D] for j in js], axis=0)
                mc = mx[rows, :]
                ps = []
                tot = sm[rows, :]
                for cg in range(span * ST // 2):
                    s = s_s[rows, pl.ds(pl.multiple_of(t * ST * BLOCK + cg * 128, 128), 128)]
                    p = jnp.exp2(s * c - mc)
                    tot = tot + p
                    ps.append(p.astype(jnp.bfloat16))
                sm[rows, :] = tot
                acc[rows, :] += jnp.dot(jnp.concatenate(ps, axis=1), v, preferred_element_type=jnp.float32)

        sb(0, FIRST)
        over_slots(sb, FIRST)
        total = jnp.sum(sm[...], axis=1, keepdims=True)
        o_ref[pl.ds(rt * R, R), :] = (acc[...] / total).astype(o_ref.dtype)
        return 0
    lax.fori_loop(0, q_ref.shape[0] // R, row_tile, 0)


def attend(tables, q, kv):
    rows, cols = q.shape
    heads = cols // D
    return pl.pallas_call(
        attn_kernel,
        grid_spec=pltpu.PrefetchScalarGridSpec(
            num_scalar_prefetch=5,
            grid=(heads,),
            in_specs=[pl.BlockSpec((rows, D), lambda h, *_: (0, h)),
                      pl.BlockSpec(memory_space=pltpu.VMEM)],
            out_specs=pl.BlockSpec((rows, D), lambda h, *_: (0, h)),
            scratch_shapes=[
                pltpu.VMEM((VERT * BLOCK, 2 * D), jnp.bfloat16),
                pltpu.VMEM((R, VERT * BLOCK), jnp.float32),
                pltpu.VMEM((R, SLOTS * BLOCK), jnp.float32),
                pltpu.VMEM((R, 128), jnp.float32),
                pltpu.VMEM((R, D), jnp.float32),
                pltpu.VMEM((R, 128), jnp.float32),
            ],
        ),
        out_shape=jax.ShapeDtypeStruct((rows, cols), jnp.bfloat16),
        compiler_params=pltpu.CompilerParams(vmem_limit_bytes=56 << 20),
    )(*tables, q, kv)


def tables_of(vertical, vert_count, slash, slash_count, blocks, context_blocks, query_blocks):
    n = vertical.shape[1]
    idx = jnp.arange(n, dtype=jnp.int32)
    live = idx[None] < vert_count[:, None]
    key = jnp.where(live, vertical, 4096 + idx[None])
    rank = jnp.sum((key[:, None, :] < key[:, :, None]).astype(jnp.int32), axis=2)
    sv = jnp.sum(jnp.where(rank[:, :, None] == idx[None, None, :], key[:, :, None], 0), axis=1)
    n_eff = jnp.sum((key < jnp.max(blocks)).astype(jnp.int32), axis=1)
    isv = jnp.sum((key[:, :, None] == jnp.arange(context_blocks, dtype=jnp.int32)[None, None]).astype(jnp.int32), axis=1)
    offs = jnp.pad(slash + 1, ((0, 0), (1, SLOTS - 1 - slash.shape[1])))
    meta = jnp.stack([n_eff, slash_count])
    return sv, isv, offs, meta, blocks


MESH_ID = pl.DeviceIdType.MESH
PEERS = 8
LATE = (5, 6, 7)


def place():
    rep = lax.axis_index("rep")
    seq = lax.axis_index("seq")
    y, x, z = seq // 16, (seq // 4) % 4, seq % 4
    ring = y * (1 - rep) + z * rep
    other = z * (1 - rep) + y * rep
    shifted = (x + rep) % 4
    half, low = shifted // 2, shifted % 2
    return rep, seq, ring, half, low, other


def seq_at(rep, ring, half, low, other):
    y = ring * (1 - rep) + other * rep
    z = other * (1 - rep) + ring * rep
    x = (2 * half + low + 4 - rep) % 4
    return y * 16 + x * 4 + z


def peer_seq(rep, ring, turn, group):
    half, other = group // 4, group % 4
    return seq_at(rep, ring, half, (turn + half) % 2, other)


def aligned(index, size):
    return pl.ds(pl.multiple_of(index * size, size), size)


def spread_kernel(keys, values, queries, kv, q_out, local_sem, first_send, first_recv, tree_send, tree_recv):
    rep, seq, ring, half, low, other = place()
    group = half * 4 + other
    turn = (low + half) % 2
    rows = keys.shape[0]
    q_rows = queries.shape[0]
    q_width = q_out.shape[1]

    peers = [(rep, peer_seq(rep, ring, turn, (group + d) % PEERS)) for d in range(1, PEERS)]
    neighbours = {
        "pair": (rep, seq_at(rep, ring, half, 1 - low, other)),
        "up": (rep, seq_at(rep, (ring + 1) % 4, half, low, other)),
        "down": (rep, seq_at(rep, (ring + 3) % 4, half, low, other)),
    }
    barrier = pltpu.get_barrier_semaphore()
    for device in peers + list(neighbours.values()):
        pl.semaphore_signal(barrier, inc=1, device_id=device, device_id_type=MESH_ID)
    pl.semaphore_wait(barrier, len(peers) + len(neighbours))

    def first(d, kind):
        to = (group + d) % PEERS
        source = keys if kind == 0 else values
        return pltpu.make_async_remote_copy(
            src_ref=source.at[:, aligned(to, HEAD_DIM)],
            dst_ref=kv.at[aligned(seq, rows), pl.ds(kind * HEAD_DIM, HEAD_DIM)],
            send_sem=first_send.at[d, kind],
            recv_sem=first_recv.at[d, kind],
            device_id=peers[d - 1],
            device_id_type=MESH_ID,
        )

    def first_q(d):
        to = (group + d) % PEERS
        return pltpu.make_async_remote_copy(
            src_ref=queries.at[:, aligned(to, q_width)],
            dst_ref=q_out.at[aligned(group, q_rows), :],
            send_sem=first_send.at[d, 2],
            recv_sem=first_recv.at[d, 2],
            device_id=peers[d - 1],
            device_id_type=MESH_ID,
        )

    own = [
        pltpu.make_async_copy(keys.at[:, aligned(group, HEAD_DIM)], kv.at[aligned(seq, rows), pl.ds(0, HEAD_DIM)], local_sem.at[0]),
        pltpu.make_async_copy(values.at[:, aligned(group, HEAD_DIM)], kv.at[aligned(seq, rows), pl.ds(HEAD_DIM, HEAD_DIM)], local_sem.at[1]),
        pltpu.make_async_copy(queries.at[:, aligned(group, q_width)], q_out.at[aligned(group, q_rows), :], local_sem.at[2]),
    ]
    own[0].start()
    own[1].start()
    for d in range(1, PEERS):
        first(d, 0).start()
        first(d, 1).start()
    own[2].start()
    for d in range(1, PEERS):
        first_q(d).start()

    def piece_rows(up, flip, d):
        origin_low = (low + flip) % 2
        origin_turn = (origin_low + half) % 2
        origin_ring = (ring + 4 - up) % 4
        return aligned(peer_seq(rep, origin_ring, origin_turn, (group + PEERS - d) % PEERS), rows)

    moves = {"pair": (0, 1), "up": (1, 0), "down": (3, 0)}
    sends = []

    def pass_on(up, flip, d, way):
        step_up, step_flip = moves[way]
        at = piece_rows(up, flip, d)
        copy = pltpu.make_async_remote_copy(
            src_ref=kv.at[at, :],
            dst_ref=kv.at[at, :],
            send_sem=tree_send.at[len(sends)],
            recv_sem=tree_recv.at[(up + step_up) % 4, (flip + step_flip) % 2, d],
            device_id=neighbours[way],
            device_id_type=MESH_ID,
        )
        copy.start()
        sends.append(copy)

    def arrived(up, flip, d):
        at = piece_rows(up, flip, d)
        pltpu.make_async_remote_copy(
            src_ref=kv.at[at, :],
            dst_ref=kv.at[at, :],
            send_sem=tree_send.at[0],
            recv_sem=tree_recv.at[up, flip, d],
            device_id=neighbours["pair"],
            device_id_type=MESH_ID,
        ).wait_recv()

    actions = []
    for d in range(PEERS):
        onward = "up" if d % 2 == 0 else "down"
        turning = 1 if d % 2 == 0 else 3
        late = d in LATE
        actions.append((d, 0, 0, d, ["up", "down", "pair"]))
        for up in (1, 3):
            ways = [onward] if up == turning else []
            actions.append((d + 1, up, 0, d, ways + (["pair"] if late else [])))
            actions.append((d + 2, up, 1, d, [] if late else ways))
        actions.append((d + 2, 2, 0, d, ["pair"] if late else []))
        actions.append((d + 1, 0, 1, d, [] if late else ["up", "down"]))
        actions.append((d + 3, 2, 1, d, []))
    ends = [a for a in actions if not a[4]]
    for _, up, flip, d, ways in sorted(a for a in actions if a[4]):
        if (up, flip) != (0, 0):
            arrived(up, flip, d)
        elif d == 0:
            own[0].wait()
            own[1].wait()
        else:
            first(d, 0).wait_recv()
            first(d, 1).wait_recv()
        for way in ways:
            pass_on(up, flip, d, way)
    for _, up, flip, d, _ in ends:
        arrived(up, flip, d)
    own[2].wait()
    for d in range(1, PEERS):
        first_q(d).wait_recv()
    for d in range(1, PEERS):
        first(d, 0).wait_send()
        first(d, 1).wait_send()
        first_q(d).wait_send()
    for copy in sends:
        copy.wait_send()


def spread(keys, values, queries):
    seq_count = lax.axis_size("seq")
    any_space = pl.BlockSpec(memory_space=pl.ANY)
    return pl.pallas_call(
        spread_kernel,
        out_shape=(
            jax.ShapeDtypeStruct((seq_count * keys.shape[0], 2 * HEAD_DIM), keys.dtype),
            jax.ShapeDtypeStruct((PEERS * queries.shape[0], queries.shape[1] // PEERS), queries.dtype),
        ),
        in_specs=[any_space] * 3,
        out_specs=(any_space, any_space),
        scratch_shapes=[
            pltpu.SemaphoreType.DMA((3,)),
            pltpu.SemaphoreType.DMA((PEERS, 3)),
            pltpu.SemaphoreType.DMA((PEERS, 3)),
            pltpu.SemaphoreType.DMA((56,)),
            pltpu.SemaphoreType.DMA((4, 2, PEERS)),
        ],
        compiler_params=pltpu.CompilerParams(collective_id=0, has_side_effects=True),
        name="spread",
    )(keys, values, queries)


def give_back_kernel(result, out, local_sem, send_sem, recv_sem):
    rep, seq, ring, half, low, other = place()
    group = half * 4 + other
    turn = (low + half) % 2
    rows, width = out.shape[0], result.shape[1]
    peers = [(rep, peer_seq(rep, ring, turn, (group + d) % PEERS)) for d in range(1, PEERS)]
    barrier = pltpu.get_barrier_semaphore()
    for device in peers:
        pl.semaphore_signal(barrier, inc=1, device_id=device, device_id_type=MESH_ID)
    pl.semaphore_wait(barrier, len(peers))
    copies = []
    for d in range(1, PEERS):
        copy = pltpu.make_async_remote_copy(
            src_ref=result.at[aligned((group + d) % PEERS, rows), :],
            dst_ref=out.at[:, aligned(group, width)],
            send_sem=send_sem.at[d],
            recv_sem=recv_sem.at[d],
            device_id=peers[d - 1],
            device_id_type=MESH_ID,
        )
        copy.start()
        copies.append(copy)
    own = pltpu.make_async_copy(result.at[aligned(group, rows), :], out.at[:, aligned(group, width)], local_sem)
    own.start()
    own.wait()
    for d in range(1, PEERS):
        pltpu.make_async_remote_copy(
            src_ref=result.at[aligned((group + d) % PEERS, rows), :],
            dst_ref=out.at[:, aligned((group + PEERS - d) % PEERS, width)],
            send_sem=send_sem.at[d],
            recv_sem=recv_sem.at[d],
            device_id=peers[d - 1],
            device_id_type=MESH_ID,
        ).wait_recv()
    for copy in copies:
        copy.wait_send()


def give_back(result, rows):
    any_space = pl.BlockSpec(memory_space=pl.ANY)
    return pl.pallas_call(
        give_back_kernel,
        out_shape=jax.ShapeDtypeStruct((rows, PEERS * result.shape[1]), result.dtype),
        in_specs=[any_space],
        out_specs=any_space,
        scratch_shapes=[
            pltpu.SemaphoreType.DMA,
            pltpu.SemaphoreType.DMA((PEERS,)),
            pltpu.SemaphoreType.DMA((PEERS,)),
        ],
        compiler_params=pltpu.CompilerParams(collective_id=1, has_side_effects=True),
        name="give_back",
    )(result)


def body(queries, keys, values, vertical, vert_count, slash, slash_count):
    rep, seq, ring, half, low, other = place()
    group = half * 4 + other
    turn = (low + half) % 2
    query_rows = queries.shape[0]
    per_device = query_rows // BLOCK
    seq_count = lax.axis_size("seq")
    context_blocks = seq_count * keys.shape[0] // BLOCK
    stretch_blocks = seq_count * per_device
    sources = peer_seq(rep, ring, turn, jnp.arange(PEERS, dtype=jnp.int32))
    blocks = (context_blocks - stretch_blocks + per_device * sources[:, None] + jnp.arange(per_device, dtype=jnp.int32)[None]).reshape(-1)
    per_group = vertical.shape[0] // KV_HEADS

    def mine(x):
        return lax.dynamic_slice_in_dim(x, group * per_group, per_group, 0)

    tables = tables_of(mine(vertical), mine(vert_count), mine(slash), mine(slash_count), blocks, context_blocks, stretch_blocks)
    kv, q = spread(keys, values, queries)
    return give_back(attend(tables, q, kv), query_rows)


def solution(mesh):
    return jax.shard_map(
        body,
        mesh=mesh,
        in_specs=(
            P(("rep", "seq"), None),
            P(("rep", "seq"), None),
            P(("rep", "seq"), None),
            P("rep", None),
            P("rep"),
            P("rep", None),
            P("rep"),
        ),
        out_specs=P(("rep", "seq"), None),
        check_vma=False,
    )
```

```python
import functools, math
import jax, jax.numpy as jnp
from jax import lax
from jax.experimental import pallas as pl
from jax.experimental.pallas import tpu as pltpu
from jax.sharding import PartitionSpec as P

KV_HEADS = 8
HEAD_DIM = 128
D = HEAD_DIM
BLOCK = 64
VERT = 64
FAR = 1 << 20
SLOTS = 40
VT = 8
ST = 4
R = 1024
SPANS = (4, 2, 1)
FIRST = 2
SLASH_SPANS = (4, 2, 1)
NEG=float("-inf")

MESH_ID = pl.DeviceIdType.MESH
PEERS = 8
LATE = (5, 7)


def place():
    rep = lax.axis_index("rep")
    seq = lax.axis_index("seq")
    y, x, z = seq // 16, (seq // 4) % 4, seq % 4
    ring = y * (1 - rep) + z * rep
    other = z * (1 - rep) + y * rep
    shifted = (x + rep) % 4
    half, low = shifted // 2, shifted % 2
    return rep, seq, ring, half, low, other


def seq_at(rep, ring, half, low, other):
    y = ring * (1 - rep) + other * rep
    z = other * (1 - rep) + ring * rep
    x = (2 * half + low + 4 - rep) % 4
    return y * 16 + x * 4 + z


def peer_seq(rep, ring, turn, group):
    half, other = group // 4, group % 4
    return seq_at(rep, ring, half, (turn + half) % 2, other)


def aligned(index, size):
    return pl.ds(pl.multiple_of(index * size, size), size)


def attn_kernel(first_block, vertical, vert_count, slash, slash_count, q_ref, kv_ref, o_ref, covered, kvv, s_v, s_s, mx, acc, sm):
    rep, seq, ring, half, low, other = place()
    h = (half * 4 + other) * pl.num_programs(0) + pl.program_id(0)
    nv, ns = vert_count[h], slash_count[h]
    vtiles = (nv + VT - 1) // VT
    per_device = q_ref.shape[0] // BLOCK // PEERS
    stiles = (ns + 1 + ST - 1) // ST
    c = math.log2(math.e) / math.sqrt(D)

    @pl.when(pl.program_id(0) == 0)
    def _():
        def clear(i, _):
            for u in range(8):
                covered[i * 8 + u] = 0
            return 0
        lax.fori_loop(0, kv_ref.shape[0] // BLOCK // 8, clear, 0)

    def gather(i, _):
        for u in range(VT):
            b = vertical[h, i * VT + u]
            covered[b] = jnp.where(i * VT + u < nv, 1, 0)
            kvv[pl.ds((i * VT + u) * BLOCK, BLOCK), :] = kv_ref[pl.ds(b * BLOCK, BLOCK), :]
        return 0
    lax.fori_loop(0, vtiles, gather, 0)
    lane = lax.broadcasted_iota(jnp.int32, (1, 128), 1)
    left = lane < BLOCK
    nsub = R // BLOCK

    def two(x, y):
        return jnp.where(left, x, y)

    def row_tile(rt, _):
        q = q_ref[pl.ds(rt * R, R), :]
        blocks = [first_block + per_device * peer_seq(rep, ring, (low + half) % 2, i // per_device) + i % per_device for i in range(nsub)]
        mx[...] = jnp.full_like(mx, NEG)

        def va(t, span):
            keys = span * VT * BLOCK
            at = pl.ds(pl.multiple_of(t * VT * BLOCK, VT * BLOCK), keys)
            s = lax.dot_general(q, kvv[at, 0:D], (((1,), (1,)), ((), ())), preferred_element_type=jnp.float32)
            ids = [jnp.where(t * VT + u < nv, vertical[h, t * VT + u], FAR) for u in range(span * VT)]
            rows = []
            for i in range(nsub):
                cols = []
                for cg in range(span * VT // 2):
                    b = two(jnp.where(ids[2 * cg] < blocks[i], 0.0, NEG), jnp.where(ids[2 * cg + 1] < blocks[i], 0.0, NEG))
                    cols.append(s[i * BLOCK:(i + 1) * BLOCK, cg * 128:(cg + 1) * 128] + b)
                rows.append(jnp.concatenate(cols, axis=1))
            s = jnp.concatenate(rows, axis=0)
            s_v[:, at] = s
            m = s[:, 0:128]
            for cg in range(1, span * VT // 2):
                m = jnp.maximum(m, s[:, cg * 128:(cg + 1) * 128])
            mx[...] = jnp.maximum(mx[...], m)

        def over_tiles(step):
            done = 0
            for span in SPANS:
                count = (vtiles - done) // span
                lax.fori_loop(0, count, lambda n, _, done=done, span=span: (step(done + n * span, span), 0)[1], 0)
                done = done + count * span

        over_tiles(va)

        def entry(k):
            last = slash.shape[1] - 1
            return min(k, last) if isinstance(k, int) else jnp.minimum(k, last)

        def slots_of(t, i, span, own):
            return [blocks[i] if own and u == 0 else blocks[i] - 1 - slash[h, entry(t * ST + u - 1)] for u in range(span * ST)]

        def sa(t, span, first=False):
            for i in range(nsub):
                js = slots_of(t, i, span, first)
                k = jnp.concatenate([kv_ref[pl.ds(j * BLOCK, BLOCK), 0:D] for j in js], axis=0)
                s = lax.dot_general(q[i * BLOCK:(i + 1) * BLOCK], k, (((1,), (1,)), ((), ())), preferred_element_type=jnp.float32)
                m = mx[i * BLOCK:(i + 1) * BLOCK, :]
                for cg in range(span * ST // 2):
                    bias = []
                    for u in (2 * cg, 2 * cg + 1):
                        dead = jnp.where(t * ST + u <= ns, covered[js[u]], 1)
                        if first and u == 0:
                            dead = 0
                        bias.append(jnp.where(dead == 0, 0.0, NEG))
                    part = s[:, cg * 128:(cg + 1) * 128] + two(*bias)
                    if first and cg == 0:
                        ri = lax.broadcasted_iota(jnp.int32, (BLOCK, 128), 0)
                        ci = lax.broadcasted_iota(jnp.int32, (BLOCK, 128), 1)
                        part = jnp.where((ci >= BLOCK) | (ri >= ci), part, NEG)
                    s_s[i * BLOCK:(i + 1) * BLOCK, pl.ds(pl.multiple_of(t * ST * BLOCK + cg * 128, 128), 128)] = part
                    m = jnp.maximum(m, part)
                mx[i * BLOCK:(i + 1) * BLOCK, :] = m

        def over_slots(step, done):
            for span in SLASH_SPANS:
                count = jnp.maximum(stiles - done, 0) // span
                lax.fori_loop(0, count, lambda n, _, done=done, span=span: (step(done + n * span, span), 0)[1], 0)
                done = done + count * span

        sa(0, FIRST, True)
        over_slots(sa, FIRST)

        mrow = jnp.max(mx[...], axis=1, keepdims=True)
        mx[...] = jnp.broadcast_to(mrow * c, (R, 128))
        sm[...] = jnp.zeros_like(sm)
        acc[...] = jnp.zeros_like(acc)

        def vb(t, span):
            keys = span * VT * BLOCK
            v = kvv[pl.ds(pl.multiple_of(t * VT * BLOCK, VT * BLOCK), keys), D:2 * D]
            mc = mx[...]
            ps = []
            tot = None
            for cg in range(keys // 128):
                s = s_v[:, pl.ds(pl.multiple_of(t * VT * BLOCK + cg * 128, 128), 128)]
                p = jnp.exp2(s * c - mc)
                tot = p if tot is None else tot + p
                ps.append(p.astype(jnp.bfloat16))
            sm[...] += tot
            acc[...] += jnp.dot(jnp.concatenate(ps, axis=1), v, preferred_element_type=jnp.float32)
        over_tiles(vb)

        def sb(t, span, first=False):
            for i in range(nsub):
                js = slots_of(t, i, span, first)
                rows = slice(i * BLOCK, (i + 1) * BLOCK)
                v = jnp.concatenate([kv_ref[pl.ds(j * BLOCK, BLOCK), D:2 * D] for j in js], axis=0)
                mc = mx[rows, :]
                ps = []
                tot = sm[rows, :]
                for cg in range(span * ST // 2):
                    s = s_s[rows, pl.ds(pl.multiple_of(t * ST * BLOCK + cg * 128, 128), 128)]
                    p = jnp.exp2(s * c - mc)
                    tot = tot + p
                    ps.append(p.astype(jnp.bfloat16))
                sm[rows, :] = tot
                acc[rows, :] += jnp.dot(jnp.concatenate(ps, axis=1), v, preferred_element_type=jnp.float32)

        sb(0, FIRST, True)
        over_slots(sb, FIRST)
        total = jnp.sum(sm[...], axis=1, keepdims=True)
        o_ref[pl.ds(rt * R, R), :] = (acc[...] / total).astype(o_ref.dtype)
        return 0
    lax.fori_loop(0, q_ref.shape[0] // R, row_tile, 0)

    def uncover(i, _):
        for u in range(VT):
            covered[vertical[h, i * VT + u]] = 0
        return 0
    lax.fori_loop(0, vtiles, uncover, 0)


def attend(first_block, tables, q, kv):
    rows, cols = q.shape
    heads = cols // D
    return pl.pallas_call(
        functools.partial(attn_kernel, first_block),
        grid_spec=pltpu.PrefetchScalarGridSpec(
            num_scalar_prefetch=4,
            grid=(heads,),
            in_specs=[pl.BlockSpec((rows, D), lambda h, *_: (0, h)),
                      pl.BlockSpec(memory_space=pltpu.VMEM)],
            out_specs=pl.BlockSpec((rows, D), lambda h, *_: (0, h)),
            scratch_shapes=[
                pltpu.SMEM((kv.shape[0] // BLOCK,), jnp.int32),
                pltpu.VMEM((VERT * BLOCK, 2 * D), jnp.bfloat16),
                pltpu.VMEM((R, VERT * BLOCK), jnp.float32),
                pltpu.VMEM((R, SLOTS * BLOCK), jnp.float32),
                pltpu.VMEM((R, 128), jnp.float32),
                pltpu.VMEM((R, D), jnp.float32),
                pltpu.VMEM((R, 128), jnp.float32),
            ],
        ),
        out_shape=jax.ShapeDtypeStruct((rows, cols), jnp.bfloat16),
        compiler_params=pltpu.CompilerParams(vmem_limit_bytes=56 << 20),
    )(*tables, q, kv)


def spread_kernel(keys, values, queries, kv, q_out, local_sem, first_send, first_recv, tree_send, tree_recv):
    rep, seq, ring, half, low, other = place()
    group = half * 4 + other
    turn = (low + half) % 2
    rows = keys.shape[0]
    q_rows = queries.shape[0]
    q_width = q_out.shape[1]

    peers = [(rep, peer_seq(rep, ring, turn, (group + d) % PEERS)) for d in range(1, PEERS)]
    neighbours = {
        "pair": (rep, seq_at(rep, ring, half, 1 - low, other)),
        "up": (rep, seq_at(rep, (ring + 1) % 4, half, low, other)),
        "down": (rep, seq_at(rep, (ring + 3) % 4, half, low, other)),
    }
    barrier = pltpu.get_barrier_semaphore()
    for device in peers + list(neighbours.values()):
        pl.semaphore_signal(barrier, inc=1, device_id=device, device_id_type=MESH_ID)
    pl.semaphore_wait(barrier, len(peers) + len(neighbours))

    def first(d, kind):
        to = (group + d) % PEERS
        source = keys if kind == 0 else values
        return pltpu.make_async_remote_copy(
            src_ref=source.at[:, aligned(to, HEAD_DIM)],
            dst_ref=kv.at[aligned(seq, rows), pl.ds(kind * HEAD_DIM, HEAD_DIM)],
            send_sem=first_send.at[d, kind],
            recv_sem=first_recv.at[d, kind],
            device_id=peers[d - 1],
            device_id_type=MESH_ID,
        )

    def first_q(d):
        to = (group + d) % PEERS
        return pltpu.make_async_remote_copy(
            src_ref=queries.at[:, aligned(to, q_width)],
            dst_ref=q_out.at[aligned(group, q_rows), :],
            send_sem=first_send.at[d, 2],
            recv_sem=first_recv.at[d, 2],
            device_id=peers[d - 1],
            device_id_type=MESH_ID,
        )

    own = [
        pltpu.make_async_copy(keys.at[:, aligned(group, HEAD_DIM)], kv.at[aligned(seq, rows), pl.ds(0, HEAD_DIM)], local_sem.at[0]),
        pltpu.make_async_copy(values.at[:, aligned(group, HEAD_DIM)], kv.at[aligned(seq, rows), pl.ds(HEAD_DIM, HEAD_DIM)], local_sem.at[1]),
        pltpu.make_async_copy(queries.at[:, aligned(group, q_width)], q_out.at[aligned(group, q_rows), :], local_sem.at[2]),
    ]
    own[0].start()
    own[1].start()
    for d in range(1, PEERS):
        first(d, 0).start()
        first(d, 1).start()
    own[2].start()
    for d in range(1, PEERS):
        first_q(d).start()

    def piece_rows(up, flip, d):
        origin_low = (low + flip) % 2
        origin_turn = (origin_low + half) % 2
        origin_ring = (ring + 4 - up) % 4
        return aligned(peer_seq(rep, origin_ring, origin_turn, (group + PEERS - d) % PEERS), rows)

    moves = {"pair": (0, 1), "up": (1, 0), "down": (3, 0)}
    sends = []

    def pass_on(up, flip, d, way):
        step_up, step_flip = moves[way]
        at = piece_rows(up, flip, d)
        copy = pltpu.make_async_remote_copy(
            src_ref=kv.at[at, :],
            dst_ref=kv.at[at, :],
            send_sem=tree_send.at[len(sends)],
            recv_sem=tree_recv.at[(up + step_up) % 4, (flip + step_flip) % 2, d],
            device_id=neighbours[way],
            device_id_type=MESH_ID,
        )
        copy.start()
        sends.append(copy)

    def arrived(up, flip, d):
        at = piece_rows(up, flip, d)
        pltpu.make_async_remote_copy(
            src_ref=kv.at[at, :],
            dst_ref=kv.at[at, :],
            send_sem=tree_send.at[0],
            recv_sem=tree_recv.at[up, flip, d],
            device_id=neighbours["pair"],
            device_id_type=MESH_ID,
        ).wait_recv()

    actions = []
    for d in range(PEERS):
        onward = "up" if d % 2 == 0 else "down"
        turning = 1 if d % 2 == 0 else 3
        late = d in LATE
        actions.append((d, 0, 0, d, ["up", "down", "pair"]))
        for up in (1, 3):
            ways = [onward] if up == turning else []
            actions.append((d + 1, up, 0, d, ways + (["pair"] if late else [])))
            actions.append((d + 2, up, 1, d, [] if late else ways))
        actions.append((d + 2, 2, 0, d, ["pair"] if late else []))
        actions.append((d + 1, 0, 1, d, [] if late else ["up", "down"]))
        actions.append((d + 3, 2, 1, d, []))
    ends = [a for a in actions if not a[4]]
    for _, up, flip, d, ways in sorted(a for a in actions if a[4]):
        if (up, flip) != (0, 0):
            arrived(up, flip, d)
        elif d == 0:
            own[0].wait()
            own[1].wait()
        else:
            first(d, 0).wait_recv()
            first(d, 1).wait_recv()
        for way in ways:
            pass_on(up, flip, d, way)
    for _, up, flip, d, _ in ends:
        arrived(up, flip, d)
    own[2].wait()
    for d in range(1, PEERS):
        first_q(d).wait_recv()
    for d in range(1, PEERS):
        first(d, 0).wait_send()
        first(d, 1).wait_send()
        first_q(d).wait_send()
    for copy in sends:
        copy.wait_send()


def spread(keys, values, queries):
    seq_count = lax.axis_size("seq")
    any_space = pl.BlockSpec(memory_space=pl.ANY)
    return pl.pallas_call(
        spread_kernel,
        out_shape=(
            jax.ShapeDtypeStruct((seq_count * keys.shape[0], 2 * HEAD_DIM), keys.dtype),
            jax.ShapeDtypeStruct((PEERS * queries.shape[0], queries.shape[1] // PEERS), queries.dtype),
        ),
        in_specs=[any_space] * 3,
        out_specs=(any_space, any_space),
        scratch_shapes=[
            pltpu.SemaphoreType.DMA((3,)),
            pltpu.SemaphoreType.DMA((PEERS, 3)),
            pltpu.SemaphoreType.DMA((PEERS, 3)),
            pltpu.SemaphoreType.DMA((56,)),
            pltpu.SemaphoreType.DMA((4, 2, PEERS)),
        ],
        compiler_params=pltpu.CompilerParams(collective_id=0, has_side_effects=True),
        name="spread",
    )(keys, values, queries)


def give_back_kernel(result, out, local_sem, send_sem, recv_sem):
    rep, seq, ring, half, low, other = place()
    group = half * 4 + other
    turn = (low + half) % 2
    rows, width = out.shape[0], result.shape[1]
    peers = [(rep, peer_seq(rep, ring, turn, (group + d) % PEERS)) for d in range(1, PEERS)]
    barrier = pltpu.get_barrier_semaphore()
    for device in peers:
        pl.semaphore_signal(barrier, inc=1, device_id=device, device_id_type=MESH_ID)
    pl.semaphore_wait(barrier, len(peers))
    copies = []
    for d in range(1, PEERS):
        copy = pltpu.make_async_remote_copy(
            src_ref=result.at[aligned((group + d) % PEERS, rows), :],
            dst_ref=out.at[:, aligned(group, width)],
            send_sem=send_sem.at[d],
            recv_sem=recv_sem.at[d],
            device_id=peers[d - 1],
            device_id_type=MESH_ID,
        )
        copy.start()
        copies.append(copy)
    own = pltpu.make_async_copy(result.at[aligned(group, rows), :], out.at[:, aligned(group, width)], local_sem)
    own.start()
    own.wait()
    for d in range(1, PEERS):
        pltpu.make_async_remote_copy(
            src_ref=result.at[aligned((group + d) % PEERS, rows), :],
            dst_ref=out.at[:, aligned((group + PEERS - d) % PEERS, width)],
            send_sem=send_sem.at[d],
            recv_sem=recv_sem.at[d],
            device_id=peers[d - 1],
            device_id_type=MESH_ID,
        ).wait_recv()
    for copy in copies:
        copy.wait_send()


def give_back(result, rows):
    any_space = pl.BlockSpec(memory_space=pl.ANY)
    return pl.pallas_call(
        give_back_kernel,
        out_shape=jax.ShapeDtypeStruct((rows, PEERS * result.shape[1]), result.dtype),
        in_specs=[any_space],
        out_specs=any_space,
        scratch_shapes=[
            pltpu.SemaphoreType.DMA,
            pltpu.SemaphoreType.DMA((PEERS,)),
            pltpu.SemaphoreType.DMA((PEERS,)),
        ],
        compiler_params=pltpu.CompilerParams(collective_id=1, has_side_effects=True),
        name="give_back",
    )(result)


def body(queries, keys, values, vertical, vert_count, slash, slash_count):
    seq_count = lax.axis_size("seq")
    context_blocks = seq_count * keys.shape[0] // BLOCK
    stretch_blocks = seq_count * queries.shape[0] // BLOCK
    kv, q = spread(keys, values, queries)
    return give_back(attend(context_blocks - stretch_blocks, (vertical, vert_count, slash, slash_count), q, kv), queries.shape[0])


def solution(mesh):
    return jax.shard_map(
        body,
        mesh=mesh,
        in_specs=(
            P(("rep", "seq"), None),
            P(("rep", "seq"), None),
            P(("rep", "seq"), None),
            P("rep", None),
            P("rep"),
            P("rep", None),
            P("rep"),
        ),
        out_specs=P(("rep", "seq"), None),
        check_vma=False,
    )
```

```python
import functools, math
import jax, jax.numpy as jnp
from jax import lax
from jax.experimental import pallas as pl
from jax.experimental.pallas import tpu as pltpu
from jax.sharding import PartitionSpec as P

KV_HEADS = 8
HEAD_DIM = 128
D = HEAD_DIM
BLOCK = 64
VERT = 64
FAR = 1 << 20
SLOTS = 40
VT = 8
ST = 4
R = 1024
SPANS = (4, 2, 1)
FIRST = 2
SLASH_SPANS = (4, 2, 1)
NEG=float("-inf")

MESH_ID = pl.DeviceIdType.MESH
PEERS = 8
LATE = (5, 7)


def place():
    rep = lax.axis_index("rep")
    seq = lax.axis_index("seq")
    y, x, z = seq // 16, (seq // 4) % 4, seq % 4
    ring = y * (1 - rep) + z * rep
    other = z * (1 - rep) + y * rep
    shifted = (x + rep) % 4
    half, low = shifted // 2, shifted % 2
    return rep, seq, ring, half, low, other


def seq_at(rep, ring, half, low, other):
    y = ring * (1 - rep) + other * rep
    z = other * (1 - rep) + ring * rep
    x = (2 * half + low + 4 - rep) % 4
    return y * 16 + x * 4 + z


def peer_seq(rep, ring, turn, group):
    half, other = group // 4, group % 4
    return seq_at(rep, ring, half, (turn + half) % 2, other)


def aligned(index, size):
    return pl.ds(pl.multiple_of(index * size, size), size)


def attn_kernel(first_block, vertical, vert_count, slash, slash_count, q_ref, kv_ref, o_ref, covered, kvv, s_v, s_s, mx, acc, sm):
    rep, seq, ring, half, low, other = place()
    h = (half * 4 + other) * pl.num_programs(0) + pl.program_id(0)
    nv, ns = vert_count[h], slash_count[h]
    vtiles = (nv + VT - 1) // VT
    per_device = q_ref.shape[0] // BLOCK // PEERS
    stiles = (ns + 1 + ST - 1) // ST
    c = math.log2(math.e) / math.sqrt(D)

    @pl.when(pl.program_id(0) == 0)
    def _():
        def clear(i, _):
            for u in range(8):
                covered[i * 8 + u] = 0
            return 0
        lax.fori_loop(0, kv_ref.shape[0] // BLOCK // 8, clear, 0)

    def gather(i, _):
        for u in range(VT):
            b = vertical[h, i * VT + u]
            covered[b] = jnp.where(i * VT + u < nv, 1, 0)
            kvv[pl.ds((i * VT + u) * BLOCK, BLOCK), :] = kv_ref[pl.ds(b * BLOCK, BLOCK), :]
        return 0
    lax.fori_loop(0, vtiles, gather, 0)
    lane = lax.broadcasted_iota(jnp.int32, (1, 128), 1)
    left = lane < BLOCK
    nsub = R // BLOCK

    def two(x, y):
        return jnp.where(left, x, y)

    def row_tile(rt, _):
        q = q_ref[pl.ds(rt * R, R), :]
        blocks = [first_block + per_device * peer_seq(rep, ring, (low + half) % 2, i // per_device) + i % per_device for i in range(nsub)]
        mx[...] = jnp.full_like(mx, NEG)

        def va(t, span):
            keys = span * VT * BLOCK
            at = pl.ds(pl.multiple_of(t * VT * BLOCK, VT * BLOCK), keys)
            s = lax.dot_general(q, kvv[at, 0:D], (((1,), (1,)), ((), ())), preferred_element_type=jnp.float32)
            ids = [jnp.where(t * VT + u < nv, vertical[h, t * VT + u], FAR) for u in range(span * VT)]
            rows = []
            for i in range(nsub):
                cols = []
                for cg in range(span * VT // 2):
                    b = two(jnp.where(ids[2 * cg] < blocks[i], 0.0, NEG), jnp.where(ids[2 * cg + 1] < blocks[i], 0.0, NEG))
                    cols.append(s[i * BLOCK:(i + 1) * BLOCK, cg * 128:(cg + 1) * 128] + b)
                rows.append(jnp.concatenate(cols, axis=1))
            s = jnp.concatenate(rows, axis=0)
            s_v[:, at] = s
            m = s[:, 0:128]
            for cg in range(1, span * VT // 2):
                m = jnp.maximum(m, s[:, cg * 128:(cg + 1) * 128])
            mx[...] = jnp.maximum(mx[...], m)

        def over_tiles(step):
            done = 0
            for span in SPANS:
                count = (vtiles - done) // span
                lax.fori_loop(0, count, lambda n, _, done=done, span=span: (step(done + n * span, span), 0)[1], 0)
                done = done + count * span

        over_tiles(va)

        def entry(k):
            last = slash.shape[1] - 1
            return min(k, last) if isinstance(k, int) else jnp.minimum(k, last)

        def slots_of(t, i, span, own):
            return [blocks[i] if own and u == 0 else blocks[i] - 1 - slash[h, entry(t * ST + u - 1)] for u in range(span * ST)]

        def sa(t, span, first=False):
            for i in range(nsub):
                js = slots_of(t, i, span, first)
                k = jnp.concatenate([kv_ref[pl.ds(j * BLOCK, BLOCK), 0:D] for j in js], axis=0)
                s = lax.dot_general(q[i * BLOCK:(i + 1) * BLOCK], k, (((1,), (1,)), ((), ())), preferred_element_type=jnp.float32)
                m = mx[i * BLOCK:(i + 1) * BLOCK, :]
                for cg in range(span * ST // 2):
                    bias = []
                    for u in (2 * cg, 2 * cg + 1):
                        dead = jnp.where(t * ST + u <= ns, covered[js[u]], 1)
                        if first and u == 0:
                            dead = 0
                        bias.append(jnp.where(dead == 0, 0.0, NEG))
                    part = s[:, cg * 128:(cg + 1) * 128] + two(*bias)
                    if first and cg == 0:
                        ri = lax.broadcasted_iota(jnp.int32, (BLOCK, 128), 0)
                        ci = lax.broadcasted_iota(jnp.int32, (BLOCK, 128), 1)
                        part = jnp.where((ci >= BLOCK) | (ri >= ci), part, NEG)
                    s_s[i * BLOCK:(i + 1) * BLOCK, pl.ds(pl.multiple_of(t * ST * BLOCK + cg * 128, 128), 128)] = part
                    m = jnp.maximum(m, part)
                mx[i * BLOCK:(i + 1) * BLOCK, :] = m

        def over_slots(step, done):
            for span in SLASH_SPANS:
                count = jnp.maximum(stiles - done, 0) // span
                lax.fori_loop(0, count, lambda n, _, done=done, span=span: (step(done + n * span, span), 0)[1], 0)
                done = done + count * span

        sa(0, FIRST, True)
        over_slots(sa, FIRST)

        mrow = jnp.max(mx[...], axis=1, keepdims=True)
        mx[...] = jnp.broadcast_to(mrow * c, (R, 128))
        sm[...] = jnp.zeros_like(sm)
        acc[...] = jnp.zeros_like(acc)

        def vb(t, span):
            keys = span * VT * BLOCK
            v = kvv[pl.ds(pl.multiple_of(t * VT * BLOCK, VT * BLOCK), keys), D:2 * D]
            mc = mx[...]
            ps = []
            tot = None
            for cg in range(keys // 128):
                s = s_v[:, pl.ds(pl.multiple_of(t * VT * BLOCK + cg * 128, 128), 128)]
                p = jnp.exp2(s * c - mc)
                tot = p if tot is None else tot + p
                ps.append(p.astype(jnp.bfloat16))
            sm[...] += tot
            acc[...] += jnp.dot(jnp.concatenate(ps, axis=1), v, preferred_element_type=jnp.float32)
        over_tiles(vb)

        def sb(t, span, first=False):
            for i in range(nsub):
                js = slots_of(t, i, span, first)
                rows = slice(i * BLOCK, (i + 1) * BLOCK)
                v = jnp.concatenate([kv_ref[pl.ds(j * BLOCK, BLOCK), D:2 * D] for j in js], axis=0)
                mc = mx[rows, :]
                ps = []
                tot = sm[rows, :]
                for cg in range(span * ST // 2):
                    s = s_s[rows, pl.ds(pl.multiple_of(t * ST * BLOCK + cg * 128, 128), 128)]
                    p = jnp.exp2(s * c - mc)
                    tot = tot + p
                    ps.append(p.astype(jnp.bfloat16))
                sm[rows, :] = tot
                acc[rows, :] += jnp.dot(jnp.concatenate(ps, axis=1), v, preferred_element_type=jnp.float32)

        sb(0, FIRST, True)
        over_slots(sb, FIRST)
        total = jnp.sum(sm[...], axis=1, keepdims=True)
        o_ref[pl.ds(rt * R, R), :] = (acc[...] / total).astype(o_ref.dtype)
        return 0
    lax.fori_loop(0, q_ref.shape[0] // R, row_tile, 0)

    def uncover(i, _):
        for u in range(VT):
            covered[vertical[h, i * VT + u]] = 0
        return 0
    lax.fori_loop(0, vtiles, uncover, 0)


def attend(first_block, tables, q, kv):
    rows, cols = q.shape
    heads = cols // D
    return pl.pallas_call(
        functools.partial(attn_kernel, first_block),
        grid_spec=pltpu.PrefetchScalarGridSpec(
            num_scalar_prefetch=4,
            grid=(heads,),
            in_specs=[pl.BlockSpec((rows, D), lambda h, *_: (0, h)),
                      pl.BlockSpec(memory_space=pltpu.VMEM)],
            out_specs=pl.BlockSpec((rows, D), lambda h, *_: (0, h)),
            scratch_shapes=[
                pltpu.SMEM((kv.shape[0] // BLOCK,), jnp.int32),
                pltpu.VMEM((VERT * BLOCK, 2 * D), jnp.bfloat16),
                pltpu.VMEM((R, VERT * BLOCK), jnp.float32),
                pltpu.VMEM((R, SLOTS * BLOCK), jnp.float32),
                pltpu.VMEM((R, 128), jnp.float32),
                pltpu.VMEM((R, D), jnp.float32),
                pltpu.VMEM((R, 128), jnp.float32),
            ],
        ),
        out_shape=jax.ShapeDtypeStruct((rows, cols), jnp.bfloat16),
        compiler_params=pltpu.CompilerParams(vmem_limit_bytes=56 << 20),
    )(*tables, q, kv)


def spread_kernel(keys, values, queries, kv, q_out, local_sem, first_send, first_recv, tree_send, tree_recv):
    rep, seq, ring, half, low, other = place()
    group = half * 4 + other
    turn = (low + half) % 2
    rows = keys.shape[0]
    q_rows = queries.shape[0]
    q_width = q_out.shape[1]

    peers = [(rep, peer_seq(rep, ring, turn, (group + d) % PEERS)) for d in range(1, PEERS)]
    neighbours = {
        "pair": (rep, seq_at(rep, ring, half, 1 - low, other)),
        "up": (rep, seq_at(rep, (ring + 1) % 4, half, low, other)),
        "down": (rep, seq_at(rep, (ring + 3) % 4, half, low, other)),
    }
    barrier = pltpu.get_barrier_semaphore()
    for device in peers + list(neighbours.values()):
        pl.semaphore_signal(barrier, inc=1, device_id=device, device_id_type=MESH_ID)
    pl.semaphore_wait(barrier, len(peers) + len(neighbours))

    def first(d, kind):
        to = (group + d) % PEERS
        source = keys if kind == 0 else values
        return pltpu.make_async_remote_copy(
            src_ref=source.at[:, aligned(to, HEAD_DIM)],
            dst_ref=kv.at[aligned(seq, rows), pl.ds(kind * HEAD_DIM, HEAD_DIM)],
            send_sem=first_send.at[d, kind],
            recv_sem=first_recv.at[d, kind],
            device_id=peers[d - 1],
            device_id_type=MESH_ID,
        )

    def first_q(d):
        to = (group + d) % PEERS
        return pltpu.make_async_remote_copy(
            src_ref=queries.at[:, aligned(to, q_width)],
            dst_ref=q_out.at[aligned(group, q_rows), :],
            send_sem=first_send.at[d, 2],
            recv_sem=first_recv.at[d, 2],
            device_id=peers[d - 1],
            device_id_type=MESH_ID,
        )

    own = [
        pltpu.make_async_copy(keys.at[:, aligned(group, HEAD_DIM)], kv.at[aligned(seq, rows), pl.ds(0, HEAD_DIM)], local_sem.at[0]),
        pltpu.make_async_copy(values.at[:, aligned(group, HEAD_DIM)], kv.at[aligned(seq, rows), pl.ds(HEAD_DIM, HEAD_DIM)], local_sem.at[1]),
        pltpu.make_async_copy(queries.at[:, aligned(group, q_width)], q_out.at[aligned(group, q_rows), :], local_sem.at[2]),
    ]
    own[0].start()
    own[1].start()
    for d in range(1, PEERS):
        first(d, 0).start()
        first(d, 1).start()
    own[2].start()
    def piece_rows(up, flip, d):
        origin_low = (low + flip) % 2
        origin_turn = (origin_low + half) % 2
        origin_ring = (ring + 4 - up) % 4
        return aligned(peer_seq(rep, origin_ring, origin_turn, (group + PEERS - d) % PEERS), rows)

    moves = {"pair": (0, 1), "up": (1, 0), "down": (3, 0)}
    sends = []

    def pass_on(up, flip, d, way):
        step_up, step_flip = moves[way]
        at = piece_rows(up, flip, d)
        copy = pltpu.make_async_remote_copy(
            src_ref=kv.at[at, :],
            dst_ref=kv.at[at, :],
            send_sem=tree_send.at[len(sends)],
            recv_sem=tree_recv.at[(up + step_up) % 4, (flip + step_flip) % 2, d],
            device_id=neighbours[way],
            device_id_type=MESH_ID,
        )
        copy.start()
        sends.append(copy)

    def arrived(up, flip, d):
        at = piece_rows(up, flip, d)
        pltpu.make_async_remote_copy(
            src_ref=kv.at[at, :],
            dst_ref=kv.at[at, :],
            send_sem=tree_send.at[0],
            recv_sem=tree_recv.at[up, flip, d],
            device_id=neighbours["pair"],
            device_id_type=MESH_ID,
        ).wait_recv()

    actions = []
    for d in range(PEERS):
        onward = "up" if d % 2 == 0 else "down"
        turning = 1 if d % 2 == 0 else 3
        late = d in LATE
        actions.append((d, 0, 0, d, ["up", "down", "pair"]))
        for up in (1, 3):
            ways = [onward] if up == turning else []
            actions.append((d + 1, up, 0, d, ways + (["pair"] if late else [])))
            actions.append((d + 2, up, 1, d, [] if late else ways))
        actions.append((d + 2, 2, 0, d, ["pair"] if late else []))
        actions.append((d + 1, 0, 1, d, [] if late else ["up", "down"]))
        actions.append((d + 3, 2, 1, d, []))
    ends = [a for a in actions if not a[4]]
    for _, up, flip, d, ways in sorted(a for a in actions if a[4]):
        if (up, flip) != (0, 0):
            arrived(up, flip, d)
        elif d == 0:
            own[0].wait()
            own[1].wait()
        else:
            first(d, 0).wait_recv()
            first(d, 1).wait_recv()
        for way in ways:
            pass_on(up, flip, d, way)
        if (up, flip, d) == (0, 0, 0):
            for to in range(1, PEERS):
                first_q(to).start()
    for _, up, flip, d, _ in ends:
        arrived(up, flip, d)
    own[2].wait()
    for d in range(1, PEERS):
        first_q(d).wait_recv()
    for d in range(1, PEERS):
        first(d, 0).wait_send()
        first(d, 1).wait_send()
        first_q(d).wait_send()
    for copy in sends:
        copy.wait_send()


def spread(keys, values, queries):
    seq_count = lax.axis_size("seq")
    any_space = pl.BlockSpec(memory_space=pl.ANY)
    return pl.pallas_call(
        spread_kernel,
        out_shape=(
            jax.ShapeDtypeStruct((seq_count * keys.shape[0], 2 * HEAD_DIM), keys.dtype),
            jax.ShapeDtypeStruct((PEERS * queries.shape[0], queries.shape[1] // PEERS), queries.dtype),
        ),
        in_specs=[any_space] * 3,
        out_specs=(any_space, any_space),
        scratch_shapes=[
            pltpu.SemaphoreType.DMA((3,)),
            pltpu.SemaphoreType.DMA((PEERS, 3)),
            pltpu.SemaphoreType.DMA((PEERS, 3)),
            pltpu.SemaphoreType.DMA((56,)),
            pltpu.SemaphoreType.DMA((4, 2, PEERS)),
        ],
        compiler_params=pltpu.CompilerParams(collective_id=0, has_side_effects=True),
        name="spread",
    )(keys, values, queries)


def give_back_kernel(result, out, local_sem, send_sem, recv_sem):
    rep, seq, ring, half, low, other = place()
    group = half * 4 + other
    turn = (low + half) % 2
    rows, width = out.shape[0], result.shape[1]
    peers = [(rep, peer_seq(rep, ring, turn, (group + d) % PEERS)) for d in range(1, PEERS)]
    barrier = pltpu.get_barrier_semaphore()
    for device in peers:
        pl.semaphore_signal(barrier, inc=1, device_id=device, device_id_type=MESH_ID)
    pl.semaphore_wait(barrier, len(peers))
    copies = []
    for d in range(1, PEERS):
        copy = pltpu.make_async_remote_copy(
            src_ref=result.at[aligned((group + d) % PEERS, rows), :],
            dst_ref=out.at[:, aligned(group, width)],
            send_sem=send_sem.at[d],
            recv_sem=recv_sem.at[d],
            device_id=peers[d - 1],
            device_id_type=MESH_ID,
        )
        copy.start()
        copies.append(copy)
    own = pltpu.make_async_copy(result.at[aligned(group, rows), :], out.at[:, aligned(group, width)], local_sem)
    own.start()
    own.wait()
    for d in range(1, PEERS):
        pltpu.make_async_remote_copy(
            src_ref=result.at[aligned((group + d) % PEERS, rows), :],
            dst_ref=out.at[:, aligned((group + PEERS - d) % PEERS, width)],
            send_sem=send_sem.at[d],
            recv_sem=recv_sem.at[d],
            device_id=peers[d - 1],
            device_id_type=MESH_ID,
        ).wait_recv()
    for copy in copies:
        copy.wait_send()


def give_back(result, rows):
    any_space = pl.BlockSpec(memory_space=pl.ANY)
    return pl.pallas_call(
        give_back_kernel,
        out_shape=jax.ShapeDtypeStruct((rows, PEERS * result.shape[1]), result.dtype),
        in_specs=[any_space],
        out_specs=any_space,
        scratch_shapes=[
            pltpu.SemaphoreType.DMA,
            pltpu.SemaphoreType.DMA((PEERS,)),
            pltpu.SemaphoreType.DMA((PEERS,)),
        ],
        compiler_params=pltpu.CompilerParams(collective_id=1, has_side_effects=True),
        name="give_back",
    )(result)


def body(queries, keys, values, vertical, vert_count, slash, slash_count):
    seq_count = lax.axis_size("seq")
    context_blocks = seq_count * keys.shape[0] // BLOCK
    stretch_blocks = seq_count * queries.shape[0] // BLOCK
    kv, q = spread(keys, values, queries)
    return give_back(attend(context_blocks - stretch_blocks, (vertical, vert_count, slash, slash_count), q, kv), queries.shape[0])


def solution(mesh):
    return jax.shard_map(
        body,
        mesh=mesh,
        in_specs=(
            P(("rep", "seq"), None),
            P(("rep", "seq"), None),
            P(("rep", "seq"), None),
            P("rep", None),
            P("rep"),
            P("rep", None),
            P("rep"),
        ),
        out_specs=P(("rep", "seq"), None),
        check_vma=False,
    )
```
